32 devices in a mesh: group: 2 (over y), polar: 8 (over z, x), azimuth: 2 (over core).
Axes of the slice: x: 2, y: 2, z: 4, core: 2. Of those that a mesh axis runs over, the one named last changes fastest.
Arguments:
- state_grid: bfloat16 [768, 1440, 256], P(('group', 'polar'), 'azimuth'), parts along dimension 0, may hold values from -6 to 6
- cotangent: bfloat16 [768, 1440, 256], P(('group', 'polar'), 'azimuth'), parts along dimension 0, may hold values from -1.1953125 to 1.1953125
- legendre: bfloat16 [384, 384, 384], P('polar'), may hold values from -0.3125 to 0.3125
- quad_weight: float32 [384], replicated, may hold values from 0.3 to 3
- spec_weight: float32 [384, 2, 256], replicated, may hold values from -6 to 6
- w_in: bfloat16 [256, 512], replicated, may hold values from -0.375 to 0.375
- w_out: bfloat16 [512, 256], replicated, may hold values from -0.25 to 0.25
- lat_order: int32 [384], replicated, may hold values from 0 to 383, each once
- m_order: int32 [384], replicated, may hold values from 0 to 383, each once
Outputs:
- block_out: bfloat16 [768, 1440, 256], P(('group', 'polar'), 'azimuth'), parts along dimension 0
- spec_grad: float32 [384, 2, 512], P('polar', None, ('group', 'azimuth')), parts along dimension 2
The draws below stay inside these ranges and needn't reach their ends.
There are 2 independent parts, one for each index of `group`. The reference program is written for one: setup_inputs(seed, part) draws one part's arguments, and reference() takes and returns one part's arrays. A program takes and returns all parts, laid end to end along the dimension named above; an argument that names none is the same for every part. Nothing has to cross between parts.
Inputs may be any that keep to these rules, and one draw needn't show every extreme that they name: A permutation of the latitudes: grid row i of state_grid, cotangent and block_out is latitude lat_order[i]. A permutation of the wavenumbers: row k of legendre is wavenumber m_order[k].
All inputs are finite; a program needn't handle non-finite values.
Results may differ from the reference program's by a relative error of at most 0.008.
Values may be sent and summed in bfloat16 or wider, within the bound.
A program may use at most 448 MiB of HBM per device.

```python
import math
from functools import partial
import jax
import jax.numpy as jnp
from jax import lax

NLAT = 384
NLON = 1440
M = 384
C = 256
HID = 512


def level_of(own_key, dims, split, low, high):
    loudness = 1.0
    for position, shards_of in split:
        heights = jax.random.uniform(jax.random.fold_in(jax.random.fold_in(own_key, 6), position), (shards_of,), jnp.float32, low / len(split), high / len(split))
        loudness = loudness * jnp.repeat(jnp.exp(heights), dims[position] // shards_of).reshape((-1,) + (1,) * (len(dims) - 1 - position))
    return loudness


def scatter_about(stream_key, shape, deviation, bound, split=(), kind=jnp.bfloat16):
    drawn = jax.random.normal(stream_key, shape, jnp.float32) * deviation
    if len(split) > 0:
        drawn = level_of(stream_key, shape, split, -0.22, 0.18) * drawn
    return jnp.clip(drawn, min=-bound, max=bound).astype(kind)


def setup_inputs(seed: int = 0, part: int = 0) -> dict:
    arg_keys = jax.random.split(jax.random.key(seed), 10)
    part_splits = jax.random.split(jax.random.fold_in(arg_keys[9], part), 10)
    state_grid = scatter_about(part_splits[0], (NLAT, NLON, C), 1.0, 6.0, ((0, 8), (1, 2)))
    cotangent = scatter_about(part_splits[1], (NLAT, NLON, C), 0.2, 1.1953125, ((0, 8), (1, 2)))
    legendre = scatter_about(arg_keys[2], (M, M, NLAT), NLAT ** -0.5, 0.3125, ((0, 8),))
    quad_weight = jnp.clip(jnp.exp(jax.random.uniform(arg_keys[3], (NLAT,), jnp.float32, math.log(0.3), math.log(3.0))), 0.3, 3.0)
    spec_weight = scatter_about(arg_keys[4], (M, 2, C), 1.0, 6.0, (), jnp.float32)
    w_in = scatter_about(arg_keys[5], (C, HID), C ** -0.5, 0.375)
    w_out = scatter_about(arg_keys[6], (HID, C), HID ** -0.5, 0.25)
    lat_order = jax.random.permutation(arg_keys[7], NLAT).astype(jnp.int32)
    m_order = jax.random.permutation(arg_keys[8], M).astype(jnp.int32)
    return {"state_grid": state_grid, "cotangent": cotangent, "legendre": legendre, "quad_weight": quad_weight, "spec_weight": spec_weight, "w_in": w_in, "w_out": w_out, "lat_order": lat_order, "m_order": m_order}


def wave_table(m_order, lon_count):
    lon_index = jnp.arange(lon_count, dtype=jnp.int32)
    phase_int = lon_index[:, None] * m_order[None, :] % lon_count
    angle_rad = phase_int.astype(jnp.float32) * (2.0 * math.pi / lon_count)
    norm_scale = 1.0 / math.sqrt(lon_count)
    return jnp.stack([jnp.cos(angle_rad) * norm_scale, -jnp.sin(angle_rad) * norm_scale], axis=1).astype(jnp.bfloat16)

def rotate(coeffs, gains):
    real_part = coeffs[:, :, 0] * gains[None, :, 0] - coeffs[:, :, 1] * gains[None, :, 1]
    imag_part = coeffs[:, :, 0] * gains[None, :, 1] + coeffs[:, :, 1] * gains[None, :, 0]
    return jnp.stack([real_part, imag_part], axis=2)

def reference(state_grid, cotangent, legendre, quad_weight, spec_weight, w_in, w_out, lat_order, m_order):
    fourier_basis = wave_table(m_order, NLON)
    basis_wide = fourier_basis.astype(jnp.float32)
    fourier = jnp.einsum('inc,ntk->kitc', state_grid.astype(jnp.float32), basis_wide)
    row_quad = jnp.take(quad_weight, lat_order)
    weighted = (fourier * row_quad[None, :, None, None]).astype(jnp.bfloat16)
    table_wide = jnp.take(legendre, lat_order, axis=2).astype(jnp.float32)
    lower_mask = (jnp.arange(M, dtype=jnp.int32)[None, :] >= m_order[:, None]).astype(jnp.float32)
    coeffs = jnp.einsum('kli,kitc->kltc', table_wide, weighted.astype(jnp.float32)) * lower_mask[:, :, None, None]
    filtered = rotate(coeffs, spec_weight).astype(jnp.bfloat16)
    grid_modes = jnp.einsum('kli,kltc->kitc', table_wide, filtered.astype(jnp.float32)).astype(jnp.bfloat16)
    spectral = jnp.einsum('kitc,ntk->inc', grid_modes.astype(jnp.float32), basis_wide).astype(jnp.bfloat16)
    mixed_grid = (state_grid.astype(jnp.float32) + spectral.astype(jnp.float32)).astype(jnp.bfloat16)
    flat_mixed = mixed_grid.reshape(-1, C)
    pre_act = jnp.dot(flat_mixed, w_in, preferred_element_type=jnp.float32)
    hidden, gelu_back = jax.vjp(partial(jax.nn.gelu, approximate=True), pre_act)
    block_out = (flat_mixed.astype(jnp.float32) + jnp.dot(hidden.astype(jnp.bfloat16), w_out, preferred_element_type=jnp.float32)).astype(jnp.bfloat16)
    flat_cot = cotangent.reshape(-1, C)
    d_hidden = jnp.dot(flat_cot, w_out.T, preferred_element_type=jnp.float32)
    d_pre = gelu_back(d_hidden)[0].astype(jnp.bfloat16)
    d_mixed = (flat_cot.astype(jnp.float32) + jnp.dot(d_pre, w_in.T, preferred_element_type=jnp.float32)).astype(jnp.bfloat16)
    d_mixed = d_mixed.reshape(NLAT, NLON, C)
    d_modes = jnp.einsum('inc,ntk->kitc', d_mixed.astype(jnp.float32), basis_wide).astype(jnp.bfloat16)
    d_filt = jnp.einsum('kli,kitc->kltc', table_wide, d_modes.astype(jnp.float32))
    grad_real = lax.optimization_barrier(jnp.sum(d_filt[:, :, 0] * coeffs[:, :, 0] + d_filt[:, :, 1] * coeffs[:, :, 1], axis=0))
    grad_imag = lax.optimization_barrier(jnp.sum(d_filt[:, :, 1] * coeffs[:, :, 0] - d_filt[:, :, 0] * coeffs[:, :, 1], axis=0))
    spec_grad = jnp.stack([grad_real, grad_imag], axis=1)
    return (block_out.reshape(NLAT, NLON, C), spec_grad)
```

```python
from functools import partial
import math

import jax
import jax.numpy as jnp
from jax import lax
from jax.sharding import PartitionSpec as P


def wave_table(m_order, lon_index, lon_count):
    phase_int = lon_index[:, None] * m_order[None, :] % lon_count
    angle_rad = phase_int.astype(jnp.float32) * (2.0 * math.pi / lon_count)
    norm_scale = 1.0 / math.sqrt(lon_count)
    return jnp.stack(
        [jnp.cos(angle_rad) * norm_scale, -jnp.sin(angle_rad) * norm_scale], axis=1
    ).astype(jnp.bfloat16)


def rotate(coeffs, gains):
    real_part = coeffs[:, :, 0] * gains[None, :, 0] - coeffs[:, :, 1] * gains[None, :, 1]
    imag_part = coeffs[:, :, 0] * gains[None, :, 1] + coeffs[:, :, 1] * gains[None, :, 0]
    return jnp.stack([real_part, imag_part], axis=2)


def local(
    state_grid, cotangent, legendre, quad_weight, spec_weight, w_in, w_out, lat_order, m_order
):
    polar_count = lax.axis_size("polar")
    az_count = lax.axis_size("azimuth")
    az_index = lax.axis_index("azimuth")
    polar_index = lax.axis_index("polar")
    rows, half_lon, channels = state_grid.shape
    full_lon = half_lon * az_count
    waves = legendre.shape[0]
    degrees = legendre.shape[1]
    row_start = polar_index * rows
    width = channels // az_count
    wave_chunks = 3 if waves % 3 == 0 else 1
    row_chunks = 3 if rows % 3 == 0 else 1
    kg = waves // wave_chunks
    rg = rows // row_chunks
    swap = [(0, 1), (1, 0)]
    gain_local = lax.dynamic_slice_in_dim(spec_weight, az_index * width, width, 2)
    lon_index = (jnp.arange(full_lon, dtype=jnp.int32) + az_index * half_lon) % full_lon
    basis = wave_table(m_order, lon_index, full_lon)
    row_lats = lax.dynamic_slice_in_dim(lat_order, row_start, rows, 0)
    row_quad = jnp.take(quad_weight, row_lats)
    waves_here = lax.dynamic_slice_in_dim(m_order, polar_index * waves, waves, 0)
    lat_pick = (jnp.arange(lat_order.shape[0], dtype=jnp.int32)[:, None] == lat_order[None, :]).astype(
        jnp.bfloat16
    )
    lower_mask = (jnp.arange(degrees, dtype=jnp.int32)[None, :] >= waves_here[:, None]).astype(
        jnp.float32
    )

    def spread(grid_in):
        own = lax.dynamic_slice_in_dim(grid_in, az_index * width, width, 2)
        other = lax.dynamic_slice_in_dim(grid_in, (1 - az_index) * width, width, 2)
        return jnp.concatenate([own, lax.ppermute(other, "azimuth", swap)], axis=1)

    def exchange(x):
        return lax.all_to_all(x, "polar", split_axis=0, concat_axis=0, tiled=True)

    lon_full = spread(state_grid)
    basis_parts = basis.reshape(full_lon, 2, polar_count, wave_chunks, kg)
    table = jnp.dot(
        legendre.reshape(waves * degrees, -1), lat_pick, preferred_element_type=jnp.float32
    ).astype(jnp.bfloat16)
    table = table.reshape(waves, degrees, polar_count, rows)

    coeffs, modes = [], []
    for g in range(wave_chunks):
        fourier = jnp.einsum(
            "rnc,ntpk->pkrtc", lon_full, basis_parts[:, :, :, g], preferred_element_type=jnp.float32
        )
        weighted = (fourier * row_quad[None, None, :, None, None]).astype(jnp.bfloat16)
        at_waves = exchange(weighted)
        part = table[g * kg : (g + 1) * kg]
        mask = lower_mask[g * kg : (g + 1) * kg]
        coeffs_g = jnp.einsum(
            "klpr,pkrtc->kltc", part, at_waves, preferred_element_type=jnp.float32
        ) * mask[:, :, None, None]
        filtered = rotate(coeffs_g, gain_local).astype(jnp.bfloat16)
        modes_g = jnp.einsum(
            "klpr,kltc->pkrtc", part, filtered, preferred_element_type=jnp.float32
        ).astype(jnp.bfloat16)
        coeffs.append(coeffs_g)
        modes.append(modes_g)

    block_outs = []
    d_filt = None
    for h in range(row_chunks):
        span = slice(h * rg, (h + 1) * rg)
        at_rows = exchange(jnp.concatenate([m[:, :, span] for m in modes], axis=1))
        at_rows = at_rows.reshape(polar_count * waves, rg, 2, width)
        spectral = jnp.einsum(
            "krtc,ntk->rnc", at_rows, basis, preferred_element_type=jnp.float32
        ).astype(jnp.bfloat16)
        own = spectral[:, :half_lon]
        came = lax.ppermute(spectral[:, half_lon:], "azimuth", swap)
        returned = jnp.where(
            az_index == 0,
            jnp.concatenate([own, came], axis=2),
            jnp.concatenate([came, own], axis=2),
        )
        mixed = (state_grid[span].astype(jnp.float32) + returned.astype(jnp.float32)).astype(
            jnp.bfloat16
        )
        flat_mixed = mixed.reshape(-1, channels)
        pre_act = jnp.dot(flat_mixed, w_in, preferred_element_type=jnp.float32)
        hidden, gelu_back = jax.vjp(partial(jax.nn.gelu, approximate=True), pre_act)
        block_out = (
            flat_mixed.astype(jnp.float32)
            + jnp.dot(hidden.astype(jnp.bfloat16), w_out, preferred_element_type=jnp.float32)
        ).astype(jnp.bfloat16)
        block_outs.append(block_out.reshape(mixed.shape))
        flat_cot = cotangent[span].reshape(-1, channels)
        d_hidden = jnp.dot(flat_cot, w_out.T, preferred_element_type=jnp.float32)
        d_pre = gelu_back(d_hidden)[0].astype(jnp.bfloat16)
        d_mixed = (
            flat_cot.astype(jnp.float32)
            + jnp.dot(d_pre, w_in.T, preferred_element_type=jnp.float32)
        ).astype(jnp.bfloat16)
        d_full = spread(d_mixed.reshape(mixed.shape))
        d_modes = jnp.einsum(
            "rnc,ntk->krtc", d_full, basis, preferred_element_type=jnp.float32
        ).astype(jnp.bfloat16)
        d_waves = exchange(d_modes.reshape(polar_count, waves, rg, 2, width))
        d_part = jnp.einsum(
            "klpr,pkrtc->kltc", table[:, :, :, span], d_waves, preferred_element_type=jnp.float32
        )
        d_filt = d_part if d_filt is None else d_filt + d_part

    grad_real, grad_imag = 0.0, 0.0
    for g in range(wave_chunks):
        c, d = coeffs[g], d_filt[g * kg : (g + 1) * kg]
        grad_real += jnp.sum(d[:, :, 0] * c[:, :, 0] + d[:, :, 1] * c[:, :, 1], axis=0)
        grad_imag += jnp.sum(d[:, :, 1] * c[:, :, 0] - d[:, :, 0] * c[:, :, 1], axis=0)
    grad_terms = jnp.stack([grad_real, grad_imag], axis=1)
    shares = exchange(grad_terms.reshape(polar_count, degrees // polar_count, 2, width))
    spec_grad = jnp.sum(shares, axis=0)
    return (jnp.concatenate(block_outs, axis=0), spec_grad)


def solution(mesh):
    return jax.shard_map(
        local,
        mesh=mesh,
        in_specs=(
            P(("group", "polar"), "azimuth", None),
            P(("group", "polar"), "azimuth", None),
            P("polar", None, None),
            P(),
            P(),
            P(),
            P(),
            P(),
            P(),
        ),
        out_specs=(P(("group", "polar"), "azimuth", None), P("polar", None, ("group", "azimuth"))),
        check_vma=False,
    )
```

```python
from functools import partial
import math

import jax
import jax.numpy as jnp
from jax import lax
from jax.experimental import pallas as pl
from jax.experimental.pallas import tpu as pltpu
from jax.sharding import PartitionSpec as P


def wave_table(m_order, lon_index, lon_count):
    phase_int = lon_index[:, None] * m_order[None, :] % lon_count
    angle_rad = phase_int.astype(jnp.float32) * (2.0 * math.pi / lon_count)
    norm_scale = 1.0 / math.sqrt(lon_count)
    return jnp.stack(
        [jnp.cos(angle_rad) * norm_scale, -jnp.sin(angle_rad) * norm_scale], axis=1
    ).astype(jnp.bfloat16)


def rotate(coeffs, gains):
    real_part = coeffs[:, 0] * gains[None, 0] - coeffs[:, 1] * gains[None, 1]
    imag_part = coeffs[:, 0] * gains[None, 1] + coeffs[:, 1] * gains[None, 0]
    return jnp.stack([real_part, imag_part], axis=1)


GELU_SCALE = math.sqrt(2.0 / math.pi)
GELU_CUBIC = 0.044715


def mlp_body(
    pieces, az_ref, state_ref, own_ref, came_ref, cot_ref, w_in_ref, w_out_ref, w_out_t_ref,
    w_in_t_ref, *rest
):
    out_ref, d_own_ref, d_other_ref = rest[-3:]
    first = az_ref[0] == 0
    width = own_ref.shape[-1]
    step = state_ref.shape[1] // pieces
    for p in range(pieces):
        at = slice(p * step, (p + 1) * step)
        own = own_ref[0, at].astype(jnp.float32)
        came = came_ref[0, at].astype(jnp.float32)
        spectral = jnp.concatenate(
            [jnp.where(first, own, came), jnp.where(first, came, own)], axis=1
        )
        mixed = (state_ref[0, at].astype(jnp.float32) + spectral).astype(jnp.bfloat16)
        cot = cot_ref[0, at]
        x = jnp.dot(mixed, w_in_ref[...], preferred_element_type=jnp.float32)
        d_hidden = jnp.dot(cot, w_out_t_ref[...], preferred_element_type=jnp.float32)
        square = x * x
        t = jnp.tanh(x * (GELU_SCALE + (GELU_SCALE * GELU_CUBIC) * square))
        half = 0.5 * x
        hidden = (half + half * t).astype(jnp.bfloat16)
        slope = GELU_SCALE + (3.0 * GELU_SCALE * GELU_CUBIC) * square
        rise = 0.5 + 0.5 * t + half * (1.0 - t * t) * slope
        d_pre = (d_hidden * rise).astype(jnp.bfloat16)
        out_ref[0, at] = (
            mixed.astype(jnp.float32)
            + jnp.dot(hidden, w_out_ref[...], preferred_element_type=jnp.float32)
        ).astype(jnp.bfloat16)
        d_mixed = cot.astype(jnp.float32) + jnp.dot(
            d_pre, w_in_t_ref[...], preferred_element_type=jnp.float32
        )
        low, high = d_mixed[:, :width], d_mixed[:, width:]
        d_own_ref[0, at] = jnp.where(first, low, high).astype(jnp.bfloat16)
        d_other_ref[0, at] = jnp.where(first, high, low).astype(jnp.bfloat16)


def mlp(start, az_index, state_grid, spectral, came, cotangent, w_in, w_out, block_out):
    rows, half_lon, channels = state_grid.shape
    rg, _, width = came.shape
    hid = w_in.shape[1]
    pieces = 3 if half_lon % 48 == 0 else 1
    field = pl.BlockSpec((1, half_lon, channels), lambda i: (start + i, 0, 0))
    part = pl.BlockSpec((1, half_lon, width), lambda i: (i, 0, 0))
    whole = lambda a: pl.BlockSpec(a.shape, lambda i: (0, 0))
    w_out_t, w_in_t = w_out.T, w_in.T
    operands = [az_index.reshape(1), state_grid, spectral, came, cotangent, w_in, w_out, w_out_t, w_in_t]
    in_specs = [
        pl.BlockSpec(memory_space=pltpu.SMEM), field, part, part, field,
        whole(w_in), whole(w_out), whole(w_out_t), whole(w_in_t),
    ]
    aliases = {}
    if block_out is not None:
        aliases = {len(operands): 0}
        operands.append(block_out)
        in_specs.append(pl.BlockSpec(memory_space=pl.ANY))
    half = jax.ShapeDtypeStruct((rg, half_lon, width), jnp.bfloat16)
    tokens = rg * half_lon
    return pl.pallas_call(
        partial(mlp_body, pieces),
        grid=(rg,),
        in_specs=in_specs,
        out_specs=[field, part, part],
        out_shape=[jax.ShapeDtypeStruct(state_grid.shape, jnp.bfloat16), half, half],
        input_output_aliases=aliases,
        compiler_params=pltpu.CompilerParams(vmem_limit_bytes=48 * 1024 * 1024),
        cost_estimate=pl.CostEstimate(
            flops=8 * tokens * channels * hid,
            bytes_accessed=10 * tokens * channels,
            transcendentals=tokens * hid,
        ),
    )(*operands)


def gather_body(table_ref, modes_ref, coeffs_ref, out_ref):
    @pl.when(pl.program_id(0) == 0)
    def _():
        out_ref[...] = jnp.zeros_like(out_ref)

    real, imag = out_ref[0], out_ref[1]
    for j in range(table_ref.shape[0]):
        both = jnp.concatenate([modes_ref[:, j, 0], modes_ref[:, j, 1]], axis=2)
        both = both.reshape(both.shape[0] * both.shape[1], both.shape[2])
        d_filt = jnp.dot(table_ref[j], both, preferred_element_type=jnp.float32)
        width = d_filt.shape[1] // 2
        d0, d1 = d_filt[:, :width], d_filt[:, width:]
        c0, c1 = coeffs_ref[j, 0], coeffs_ref[j, 1]
        real += d0 * c0 + d1 * c1
        imag += d1 * c0 - d0 * c1
    out_ref[0] = real
    out_ref[1] = imag


def filter_terms(table_h, d_waves, coeffs):
    waves, degrees, lats = table_h.shape
    shards, _, _, rg, width = d_waves.shape
    if rg % 16 != 0:
        part = table_h.reshape(waves, degrees, shards, rg)
        d = jnp.einsum("klpr,pktrc->ktlc", part, d_waves, preferred_element_type=jnp.float32)
        real = jnp.sum(d[:, 0] * coeffs[:, 0] + d[:, 1] * coeffs[:, 1], axis=0)
        imag = jnp.sum(d[:, 1] * coeffs[:, 0] - d[:, 0] * coeffs[:, 1], axis=0)
        return jnp.stack([real, imag], axis=0)
    kb = 4 if waves % 4 == 0 else 1
    return pl.pallas_call(
        gather_body,
        grid=(waves // kb,),
        in_specs=[
            pl.BlockSpec((kb, degrees, lats), lambda i: (i, 0, 0)),
            pl.BlockSpec((shards, kb, 2, rg, width), lambda i: (0, i, 0, 0, 0)),
            pl.BlockSpec((kb, 2, degrees, width), lambda i: (i, 0, 0, 0)),
        ],
        out_specs=pl.BlockSpec((2, degrees, width), lambda i: (0, 0, 0)),
        out_shape=jax.ShapeDtypeStruct((2, degrees, width), jnp.float32),
        compiler_params=pltpu.CompilerParams(vmem_limit_bytes=48 * 1024 * 1024),
        cost_estimate=pl.CostEstimate(
            flops=4 * waves * degrees * lats * width,
            bytes_accessed=waves * degrees * (2 * lats + 8 * width),
            transcendentals=0,
        ),
    )(table_h, d_waves, coeffs)


def local(
    state_grid, cotangent, legendre, quad_weight, spec_weight, w_in, w_out, lat_order, m_order
):
    polar_count = lax.axis_size("polar")
    az_count = lax.axis_size("azimuth")
    az_index = lax.axis_index("azimuth")
    polar_index = lax.axis_index("polar")
    rows, half_lon, channels = state_grid.shape
    full_lon = half_lon * az_count
    waves = legendre.shape[0]
    degrees = legendre.shape[1]
    row_start = polar_index * rows
    width = channels // az_count
    row_chunks = 3 if rows % 3 == 0 else 1
    rg = rows // row_chunks
    edge = waves // 4
    wave_spans = [slice(0, edge), slice(edge, waves - edge), slice(waves - edge, waves)]
    spans = [slice(h * rg, (h + 1) * rg) for h in range(row_chunks)]
    swap = [(0, 1), (1, 0)]
    gain_local = lax.dynamic_slice_in_dim(spec_weight, az_index * width, width, 2).transpose(1, 0, 2)
    lon_index = (jnp.arange(full_lon, dtype=jnp.int32) + az_index * half_lon) % full_lon
    basis = wave_table(m_order, lon_index, full_lon)
    row_lats = lax.dynamic_slice_in_dim(lat_order, row_start, rows, 0)
    row_quad = jnp.take(quad_weight, row_lats)
    waves_here = lax.dynamic_slice_in_dim(m_order, polar_index * waves, waves, 0)
    lat_pick = (jnp.arange(lat_order.shape[0], dtype=jnp.int32)[:, None] == lat_order[None, :]).astype(
        jnp.bfloat16
    )
    lower_mask = (jnp.arange(degrees, dtype=jnp.int32)[None, :] >= waves_here[:, None]).astype(
        jnp.float32
    )

    def join(own, other):
        return jnp.concatenate([own, lax.ppermute(other, "azimuth", swap)], axis=1)

    def exchange(x):
        return lax.all_to_all(x, "polar", split_axis=0, concat_axis=0, tiled=True)

    lon_full = join(
        lax.dynamic_slice_in_dim(state_grid, az_index * width, width, 2),
        lax.dynamic_slice_in_dim(state_grid, (1 - az_index) * width, width, 2),
    )
    basis_parts = basis.reshape(full_lon, 2, polar_count, waves)
    flat_legendre = legendre.reshape(waves * degrees, -1)

    def pick(columns):
        return jnp.dot(flat_legendre, columns, preferred_element_type=jnp.float32).astype(
            jnp.bfloat16
        )

    table = pick(lat_pick).reshape(waves, degrees, polar_count, rows)
    by_row = lat_pick.reshape(-1, polar_count, rows)
    table_rows = [
        pick(by_row[:, :, span].reshape(-1, polar_count * rg)).reshape(waves, degrees, -1)
        for span in spans
    ]
    tie = lax.optimization_barrier

    arrivals = []
    for ks in wave_spans:
        fourier = jnp.einsum(
            "rnc,ntpk->pktrc", lon_full, basis_parts[..., ks], preferred_element_type=jnp.float32
        )
        weighted = (fourier * row_quad[None, None, None, :, None]).astype(jnp.bfloat16)
        arrivals.append(exchange(weighted))

    coeffs, modes = [], []
    for g, ks in enumerate(wave_spans):
        at_waves = arrivals[g]
        if g == len(wave_spans) - 1:
            at_waves, *modes = tie((at_waves, *modes))
        part = table[ks]
        coeffs_g = jnp.einsum(
            "klpr,pktrc->ktlc", part, at_waves, preferred_element_type=jnp.float32
        ) * lower_mask[ks][:, None, :, None]
        filtered = rotate(coeffs_g, gain_local).astype(jnp.bfloat16)
        modes_g = jnp.einsum(
            "klpr,ktlc->pktrc", part, filtered, preferred_element_type=jnp.float32
        ).astype(jnp.bfloat16)
        coeffs.append(coeffs_g)
        modes.append(modes_g)

    block_out = None

    def middle(h, at_rows, block_out):
        at_rows = at_rows.reshape(polar_count * waves, 2, rg, width)
        spectral = jnp.einsum(
            "ktrc,ntk->rnc", at_rows, basis, preferred_element_type=jnp.float32
        ).astype(jnp.bfloat16)
        came = lax.ppermute(spectral[:, half_lon:], "azimuth", swap)
        block_out, d_own, d_other = mlp(
            h * rg, az_index, state_grid, spectral, came, cotangent, w_in, w_out, block_out
        )
        d_modes = jnp.einsum(
            "rnc,ntk->ktrc", join(d_own, d_other), basis, preferred_element_type=jnp.float32
        ).astype(jnp.bfloat16)
        return d_modes.reshape(polar_count, waves, 2, rg, width), block_out

    outgoing = [jnp.concatenate([m[:, :, :, span] for m in modes], axis=1) for span in spans]
    all_coeffs = jnp.concatenate(coeffs, axis=0)
    if row_chunks == 3:
        at_0, at_1 = exchange(outgoing[0]), exchange(outgoing[1])
        at_0, all_coeffs = tie((at_0, all_coeffs))
        send_0, block_out = middle(0, at_0, None)
        out_2, send_0 = tie((outgoing[2], send_0))
        at_2 = exchange(out_2)
        send_1, block_out = middle(1, at_1, block_out)
        send_0, send_1 = tie((send_0, send_1))
        d_at_0 = exchange(send_0)
        send_2, block_out = middle(2, at_2, block_out)
        send_1, send_2 = tie((send_1, send_2))
        d_at_1 = exchange(send_1)
        d_at_2 = exchange(send_2)
        early = filter_terms(table_rows[0], d_at_0, all_coeffs) + filter_terms(
            table_rows[1], d_at_1, all_coeffs
        )
        d_at_2, early = tie((d_at_2, early))
        terms = early + filter_terms(table_rows[2], d_at_2, all_coeffs)
    else:
        terms = 0.0
        for h in range(row_chunks):
            send, block_out = middle(h, exchange(outgoing[h]), block_out)
            terms += filter_terms(table_rows[h], exchange(send), all_coeffs)

    shares = exchange(
        terms.reshape(2, polar_count, degrees // polar_count, width).transpose(1, 0, 2, 3)
    )
    return (block_out, jnp.sum(shares, axis=0).transpose(1, 0, 2))


def solution(mesh):
    return jax.shard_map(
        local,
        mesh=mesh,
        in_specs=(
            P(("group", "polar"), "azimuth", None),
            P(("group", "polar"), "azimuth", None),
            P("polar", None, None),
            P(),
            P(),
            P(),
            P(),
            P(),
            P(),
        ),
        out_specs=(P(("group", "polar"), "azimuth", None), P("polar", None, ("group", "azimuth"))),
        check_vma=False,
    )
```

```python
from functools import partial
import math

import jax
import jax.numpy as jnp
from jax import lax
from jax.experimental import pallas as pl
from jax.experimental.pallas import tpu as pltpu
from jax.sharding import PartitionSpec as P


def wave_table(m_order, lon_index, lon_count):
    phase_int = lon_index[:, None] * m_order[None, :] % lon_count
    angle_rad = phase_int.astype(jnp.float32) * (2.0 * math.pi / lon_count)
    norm_scale = 1.0 / math.sqrt(lon_count)
    return jnp.stack(
        [jnp.cos(angle_rad) * norm_scale, -jnp.sin(angle_rad) * norm_scale], axis=1
    ).astype(jnp.bfloat16)


def rotate(coeffs, gains):
    real_part = coeffs[:, 0] * gains[None, 0] - coeffs[:, 1] * gains[None, 1]
    imag_part = coeffs[:, 0] * gains[None, 1] + coeffs[:, 1] * gains[None, 0]
    return jnp.stack([real_part, imag_part], axis=1)


GELU_SCALE = math.sqrt(2.0 / math.pi)
GELU_CUBIC = 0.044715


def mlp_body(
    pieces, az_ref, state_ref, own_ref, came_ref, cot_ref, w_in_ref, w_out_ref, w_out_t_ref,
    w_in_t_ref, *rest
):
    out_ref, d_own_ref, d_other_ref = rest[-3:]
    first = az_ref[0] == 0
    width = own_ref.shape[-1]
    step = state_ref.shape[1] // pieces
    for p in range(pieces):
        at = slice(p * step, (p + 1) * step)
        own = own_ref[0, at].astype(jnp.float32)
        came = came_ref[0, at].astype(jnp.float32)
        spectral = jnp.concatenate(
            [jnp.where(first, own, came), jnp.where(first, came, own)], axis=1
        )
        mixed = (state_ref[0, at].astype(jnp.float32) + spectral).astype(jnp.bfloat16)
        cot = cot_ref[0, at]
        x = jnp.dot(mixed, w_in_ref[...], preferred_element_type=jnp.float32)
        d_hidden = jnp.dot(cot, w_out_t_ref[...], preferred_element_type=jnp.float32)
        square = x * x
        t = jnp.tanh(x * (GELU_SCALE + (GELU_SCALE * GELU_CUBIC) * square))
        half = 0.5 * x
        hidden = (half + half * t).astype(jnp.bfloat16)
        slope = GELU_SCALE + (3.0 * GELU_SCALE * GELU_CUBIC) * square
        rise = 0.5 + 0.5 * t + half * (1.0 - t * t) * slope
        d_pre = (d_hidden * rise).astype(jnp.bfloat16)
        out_ref[0, at] = (
            mixed.astype(jnp.float32)
            + jnp.dot(hidden, w_out_ref[...], preferred_element_type=jnp.float32)
        ).astype(jnp.bfloat16)
        d_mixed = cot.astype(jnp.float32) + jnp.dot(
            d_pre, w_in_t_ref[...], preferred_element_type=jnp.float32
        )
        low, high = d_mixed[:, :width], d_mixed[:, width:]
        d_own_ref[0, at] = jnp.where(first, low, high).astype(jnp.bfloat16)
        d_other_ref[0, at] = jnp.where(first, high, low).astype(jnp.bfloat16)


def mlp(start, az_index, state_grid, spectral, came, cotangent, w_in, w_out, block_out):
    rows, half_lon, channels = state_grid.shape
    rg, _, width = came.shape
    hid = w_in.shape[1]
    pieces = 3 if half_lon % 48 == 0 else 1
    field = pl.BlockSpec((1, half_lon, channels), lambda i: (start + i, 0, 0))
    part = pl.BlockSpec((1, half_lon, width), lambda i: (i, 0, 0))
    whole = lambda a: pl.BlockSpec(a.shape, lambda i: (0, 0))
    w_out_t, w_in_t = w_out.T, w_in.T
    operands = [az_index.reshape(1), state_grid, spectral, came, cotangent, w_in, w_out, w_out_t, w_in_t]
    in_specs = [
        pl.BlockSpec(memory_space=pltpu.SMEM), field, part, part, field,
        whole(w_in), whole(w_out), whole(w_out_t), whole(w_in_t),
    ]
    aliases = {}
    if block_out is not None:
        aliases = {len(operands): 0}
        operands.append(block_out)
        in_specs.append(pl.BlockSpec(memory_space=pl.ANY))
    half = jax.ShapeDtypeStruct((rg, half_lon, width), jnp.bfloat16)
    tokens = rg * half_lon
    return pl.pallas_call(
        partial(mlp_body, pieces),
        grid=(rg,),
        in_specs=in_specs,
        out_specs=[field, part, part],
        out_shape=[jax.ShapeDtypeStruct(state_grid.shape, jnp.bfloat16), half, half],
        input_output_aliases=aliases,
        compiler_params=pltpu.CompilerParams(vmem_limit_bytes=24 * 1024 * 1024),
        cost_estimate=pl.CostEstimate(
            flops=0, bytes_accessed=10 * tokens * channels, transcendentals=0
        ),
    )(*operands)


def gather_body(table_ref, modes_ref, coeffs_ref, out_ref):
    @pl.when(pl.program_id(0) == 0)
    def _():
        out_ref[...] = jnp.zeros_like(out_ref)

    real, imag = out_ref[0], out_ref[1]
    for j in range(table_ref.shape[0]):
        both = jnp.concatenate([modes_ref[:, j, 0], modes_ref[:, j, 1]], axis=2)
        both = both.reshape(both.shape[0] * both.shape[1], both.shape[2])
        d_filt = jnp.dot(table_ref[j], both, preferred_element_type=jnp.float32)
        width = d_filt.shape[1] // 2
        d0, d1 = d_filt[:, :width], d_filt[:, width:]
        c0, c1 = coeffs_ref[j, 0], coeffs_ref[j, 1]
        real += d0 * c0 + d1 * c1
        imag += d1 * c0 - d0 * c1
    out_ref[0] = real
    out_ref[1] = imag


def filter_terms(table_rows, h, d_waves, place, coeffs):
    waves, degrees, _ = table_rows.shape
    shards, _, _, rg, width = d_waves.shape
    lats = shards * rg
    if rg % 16 != 0 or lats % 128 != 0:
        d_waves = d_waves[:, place * waves : (place + 1) * waves]
        part = table_rows[:, :, h * lats : (h + 1) * lats].reshape(waves, degrees, shards, rg)
        d = jnp.einsum("klpr,pktrc->ktlc", part, d_waves, preferred_element_type=jnp.float32)
        real = jnp.sum(d[:, 0] * coeffs[:, 0] + d[:, 1] * coeffs[:, 1], axis=0)
        imag = jnp.sum(d[:, 1] * coeffs[:, 0] - d[:, 0] * coeffs[:, 1], axis=0)
        return jnp.stack([real, imag], axis=0)
    kb = 4 if waves % 4 == 0 else 1
    skip = place * (waves // kb)
    return pl.pallas_call(
        gather_body,
        grid=(waves // kb,),
        in_specs=[
            pl.BlockSpec((kb, degrees, lats), lambda i: (i, 0, h)),
            pl.BlockSpec((shards, kb, 2, rg, width), lambda i: (0, skip + i, 0, 0, 0)),
            pl.BlockSpec((kb, 2, degrees, width), lambda i: (i, 0, 0, 0)),
        ],
        out_specs=pl.BlockSpec((2, degrees, width), lambda i: (0, 0, 0)),
        out_shape=jax.ShapeDtypeStruct((2, degrees, width), jnp.float32),
        compiler_params=pltpu.CompilerParams(vmem_limit_bytes=12 * 1024 * 1024),
        cost_estimate=pl.CostEstimate(
            flops=0, bytes_accessed=waves * degrees * (2 * lats + 8 * width), transcendentals=0
        ),
    )(table_rows, d_waves, coeffs)


def local(
    state_grid, cotangent, legendre, quad_weight, spec_weight, w_in, w_out, lat_order, m_order
):
    polar_count = lax.axis_size("polar")
    az_count = lax.axis_size("azimuth")
    az_index = lax.axis_index("azimuth")
    polar_index = lax.axis_index("polar")
    rows, half_lon, channels = state_grid.shape
    full_lon = half_lon * az_count
    waves = legendre.shape[0]
    degrees = legendre.shape[1]
    row_start = polar_index * rows
    width = channels // az_count
    row_chunks = 3 if rows % 3 == 0 else 1
    rg = rows // row_chunks
    first, last = waves // 4, waves // 6
    wave_spans = [slice(0, first), slice(first, waves - last), slice(waves - last, waves)]
    spans = [slice(h * rg, (h + 1) * rg) for h in range(row_chunks)]
    swap = [(0, 1), (1, 0)]
    gain_local = lax.dynamic_slice_in_dim(spec_weight, az_index * width, width, 2).transpose(1, 0, 2)
    lon_index = (jnp.arange(full_lon, dtype=jnp.int32) + az_index * half_lon) % full_lon
    basis = wave_table(m_order, lon_index, full_lon)
    row_lats = lax.dynamic_slice_in_dim(lat_order, row_start, rows, 0)
    row_quad = jnp.take(quad_weight, row_lats)
    waves_here = lax.dynamic_slice_in_dim(m_order, polar_index * waves, waves, 0)
    lat_pick = (jnp.arange(lat_order.shape[0], dtype=jnp.int32)[:, None] == lat_order[None, :]).astype(
        jnp.bfloat16
    )
    lower_mask = (jnp.arange(degrees, dtype=jnp.int32)[None, :] >= waves_here[:, None]).astype(
        jnp.float32
    )

    def join(own, other):
        return jnp.concatenate([own, lax.ppermute(other, "azimuth", swap)], axis=1)

    def exchange(x):
        return lax.all_to_all(x, "polar", split_axis=0, concat_axis=0, tiled=True)

    other = lax.dynamic_slice_in_dim(state_grid, (1 - az_index) * width, width, 2)
    own_index, other = lax.optimization_barrier((az_index, other))
    lon_full = join(lax.dynamic_slice_in_dim(state_grid, own_index * width, width, 2), other)
    shard_orders = m_order.reshape(polar_count, waves)

    def pick(source, columns):
        flat = source.reshape(source.shape[0] * degrees, -1)
        return jnp.dot(flat, columns, preferred_element_type=jnp.float32).astype(jnp.bfloat16)

    by_row = lat_pick.reshape(-1, polar_count, row_chunks, rg).transpose(0, 2, 1, 3)
    table_rows = pick(legendre, by_row.reshape(lat_pick.shape)).reshape(waves, degrees, -1)
    tie = lax.optimization_barrier

    arrivals = []
    for g, ks in enumerate(wave_spans):
        lines = shard_orders[:, ks]
        part_basis = wave_table(lines.reshape(-1), lon_index, full_lon)
        fourier = jnp.einsum(
            "rnc,ntpk->pktrc",
            lon_full,
            part_basis.reshape(full_lon, 2, *lines.shape),
            preferred_element_type=jnp.float32,
        )
        weighted = (fourier * row_quad[None, None, None, :, None]).astype(jnp.bfloat16)
        if g == len(wave_spans) - 1:
            weighted, table_rows = tie((weighted, table_rows))
        arrivals.append(exchange(weighted))

    coeffs, modes = [], []
    for g, ks in enumerate(wave_spans):
        at_waves = arrivals[g]
        if g == len(wave_spans) - 1:
            at_waves, *modes = tie((at_waves, *modes))
        part = pick(legendre[ks], lat_pick).reshape(-1, degrees, polar_count, rows)
        coeffs_g = jnp.einsum(
            "klpr,pktrc->ktlc", part, at_waves, preferred_element_type=jnp.float32
        ) * lower_mask[ks][:, None, :, None]
        filtered = rotate(coeffs_g, gain_local).astype(jnp.bfloat16)
        modes_g = jnp.einsum(
            "klpr,ktlc->pktrc", part, filtered, preferred_element_type=jnp.float32
        ).astype(jnp.bfloat16)
        coeffs.append(coeffs_g)
        modes.append(modes_g)

    block_out = None

    def mix(h, at_rows, block_out):
        at_rows = at_rows.reshape(polar_count * waves, 2, rg, width)
        spectral = jnp.einsum(
            "ktrc,ntk->rnc", at_rows, basis, preferred_element_type=jnp.float32
        ).astype(jnp.bfloat16)
        came = lax.ppermute(spectral[:, half_lon:], "azimuth", swap)
        return mlp(
            h * rg, az_index, state_grid, spectral, came, cotangent, w_in, w_out, block_out
        )

    def to_modes(d_own, d_other):
        d_modes = jnp.einsum(
            "rnc,ntk->ktrc", join(d_own, d_other), basis, preferred_element_type=jnp.float32
        ).astype(jnp.bfloat16)
        return d_modes.reshape(polar_count, waves, 2, rg, width)

    outgoing = [jnp.concatenate([m[:, :, :, span] for m in modes], axis=1) for span in spans]
    all_coeffs = jnp.concatenate(coeffs, axis=0)
    if row_chunks == 3:
        at_0, all_coeffs, out_1, out_2 = tie((exchange(outgoing[0]), all_coeffs, *outgoing[1:]))
        at_1 = exchange(out_1)
        block_out, own_0, other_0 = mix(0, at_0, None)
        send_0 = to_modes(own_0, other_0)
        out_2, send_0, at_1 = tie((out_2, send_0, at_1))
        at_2 = exchange(out_2)
        block_out, own_1, other_1 = mix(1, at_1, block_out)
        send_1 = to_modes(own_1, other_1)
        at_2, send_01 = tie((at_2, jnp.concatenate([send_0, send_1], axis=1)))
        d_at_01 = exchange(send_01)
        block_out, own_2, other_2 = mix(2, at_2, block_out)
        send_2 = to_modes(own_2, other_2)
        d_at_2 = exchange(send_2)
        early = filter_terms(table_rows, 0, d_at_01, 0, all_coeffs) + filter_terms(
            table_rows, 1, d_at_01, 1, all_coeffs
        )
        d_at_2, early = tie((d_at_2, early))
        terms = early + filter_terms(table_rows, 2, d_at_2, 0, all_coeffs)
    else:
        terms = 0.0
        for h in range(row_chunks):
            block_out, own, other = mix(h, exchange(outgoing[h]), block_out)
            d_at = exchange(to_modes(own, other))
            terms += filter_terms(table_rows, h, d_at, 0, all_coeffs)

    shares = exchange(
        terms.reshape(2, polar_count, degrees // polar_count, width).transpose(1, 0, 2, 3)
    )
    return (block_out, jnp.sum(shares, axis=0).transpose(1, 0, 2))


def solution(mesh):
    return jax.shard_map(
        local,
        mesh=mesh,
        in_specs=(
            P(("group", "polar"), "azimuth", None),
            P(("group", "polar"), "azimuth", None),
            P("polar", None, None),
            P(),
            P(),
            P(),
            P(),
            P(),
            P(),
        ),
        out_specs=(P(("group", "polar"), "azimuth", None), P("polar", None, ("group", "azimuth"))),
        check_vma=False,
    )
```
